256 devices in a mesh: front: 4 (over x), row: 16 (over z, core), col: 4 (over y).
Axes of the slice: x: 4, y: 4, z: 8, core: 2. Of those that a mesh axis runs over, the one named last changes fastest.
Arguments:
- front_matrix: float32 [4, 8192, 8192], P('front', 'row', 'col'), may hold values from -1.1 to 24, as said below
- child_update: float32 [4, 4096, 4096], P('front', 'row', 'col'), may hold values from -0.6 to 2, as said below
- block_map: int32 [4, 32], P('front'), may hold values from 0 to 63, as said below
- front_order: int32 [4], P('front'), may hold values from 4096 to 8192, as said below
Outputs:
- panel_factor: float32 [4, 8192, 512], P('front', 'row')
- schur_update: float32 [4, 8192, 8192], P('front', 'row', 'col')
The draws below stay inside these ranges and needn't reach their ends.
Inputs may be any that keep to these rules, and one draw needn't show every extreme that they name: `block_map`: each front's row names 32 different front blocks. Child block b lands in front run r or (r + 1) mod 16, where r = b // 2 and a front block's run is its index // 4; the last block of every child run lands in the next run. `front_order`: multiples of 128; some front has order 8192. `front_matrix`: each front is symmetric, and the leading 1 * 512 square block of every assembled front is positive definite. `child_update`: each update matrix is symmetric.
All inputs are finite; a program needn't handle non-finite values.
Results may differ from the reference program's by a relative error of at most 0.0003.
Values sent between devices are 32-bit elements; how exact they have to be, the bound alone decides.
No kernel may reach another device: no remote copies, remote signals or barrier semaphores. Data moves between devices by JAX's collectives and lax.ppermute only.
A program may use at most 128 MiB of HBM per device.

```python
import math
import jax
import jax.numpy as jnp
from jax import lax

BLOCK = 128
FRONT = 8192
PANEL = 512
PANELS = 1
CHILD = 4096
FRONTS = 4
FRONT_BLOCKS = 64
CHILD_BLOCKS = 32
ROW_DEVICES = 16
CHILD_RUN = 2
PARENT_RUN = 4


def symmetric_draw(key, order, spread, diag_lo, diag_hi, leading, coupling):
    first, second = jax.random.split(key, 2)
    raw = jnp.clip(jax.random.normal(first, (order, order), jnp.float32), -6.0, 6.0) * spread
    offdiag = (raw + raw.T) * (1.0 / math.sqrt(2.0))
    inside = jnp.arange(order) < leading
    offdiag = offdiag + jnp.where(inside[:, None] & inside[None, :], jnp.float32(coupling), jnp.float32(0.0))
    diagonal = jnp.exp(jax.random.uniform(second, (order,), jnp.float32, math.log(diag_lo), math.log(diag_hi)))
    ident = jnp.arange(order)[:, None] == jnp.arange(order)[None, :]
    matrix = jnp.where(ident, diagonal[:, None], offdiag)
    return matrix


def draw_front_matrix(key, part):
    return lax.map(lambda number: symmetric_draw(jax.random.fold_in(key, number), FRONT, 0.05, 6.0, 12.0, PANELS * PANEL, 0.3), jnp.arange(FRONTS))


def draw_child_update(key, part):
    return lax.map(lambda number: symmetric_draw(jax.random.fold_in(key, number + 1000), CHILD, 0.03, 0.5, 1.0, 0, 0.0), jnp.arange(FRONTS))


def one_mapping(key):
    first, second = jax.random.split(key)
    child_ids = jnp.arange(CHILD_BLOCKS)
    run_ids = child_ids // CHILD_RUN
    within = child_ids % CHILD_RUN
    coin = jax.random.randint(first, (CHILD_BLOCKS,), 0, 2)
    moving = jnp.where(within == CHILD_RUN - 1, 1, jnp.where(within == 0, 0, coin))
    target = (run_ids + moving) % ROW_DEVICES
    earlier = (target[:, None] == target[None, :]) & (child_ids[None, :] < child_ids[:, None])
    ranking = jnp.sum(earlier.astype(jnp.int32), axis=1)
    orders = jax.vmap(lambda sub: jax.random.permutation(sub, PARENT_RUN))(jax.random.split(second, ROW_DEVICES))
    return (target * PARENT_RUN + orders[target, ranking]).astype(jnp.int32)


def draw_block_map(key, part):
    return jax.vmap(lambda number: one_mapping(jax.random.fold_in(key, number)))(jnp.arange(FRONTS))


def draw_front_order(key, part):
    first, second = jax.random.split(key)
    leader = jax.random.randint(first, (), 0, FRONTS)
    values = BLOCK * jax.random.randint(second, (FRONTS,), FRONT_BLOCKS // 2, FRONT_BLOCKS + 1)
    return jnp.where(jnp.arange(FRONTS) == leader, FRONT, values).astype(jnp.int32)


def setup_inputs(seed: int = 0) -> dict:
    keys = jax.random.split(jax.random.key(seed), 5)
    return {
        "front_matrix": draw_front_matrix(jax.random.fold_in(keys[4], 71), 0),
        "child_update": draw_child_update(jax.random.fold_in(keys[4], 71), 0),
        "block_map": draw_block_map(jax.random.fold_in(keys[4], 71), 0),
        "front_order": draw_front_order(jax.random.fold_in(keys[4], 71), 0),
    }


def one_front(initial, child, mapping, order_len):
    positions = (mapping[:, None] * BLOCK + jnp.arange(BLOCK)[None, :]).reshape(CHILD)
    assembled = initial.at[positions[:, None], positions[None, :]].add(child)
    live = jnp.arange(FRONT) < order_len
    current = jnp.where(live[:, None] & live[None, :], assembled, jnp.float32(0.0))
    factors = []
    for step in range(PANELS):
        low = step * PANEL
        high = low + PANEL
        lower = jnp.linalg.cholesky(current[low:high, low:high])
        panel = lax.linalg.triangular_solve(lower, current[:, low:high], left_side=False, lower=True, transpose_a=True)
        current = current - jnp.dot(panel, panel.T, precision=lax.Precision.HIGHEST)
        keep = jnp.arange(FRONT) >= high
        current = jnp.where(keep[:, None] & keep[None, :], current, jnp.float32(0.0))
        factors.append(panel)
    return (jnp.concatenate(factors, axis=1), current)

def reference(front_matrix, child_update, block_map, front_order):
    partner = jnp.bitwise_xor(jnp.arange(FRONTS), 1)
    children = child_update[partner]
    panel_factor, schur_update = lax.map(lambda items: one_front(*items), (front_matrix, children, block_map, front_order))
    return (panel_factor, schur_update)
```

```python
import jax
import jax.numpy as jnp
from jax import lax
from jax.experimental import pallas as pl
from jax.experimental.pallas import tpu as pltpu
from jax.sharding import PartitionSpec as P

BLOCK = 128
PANEL = 512
FRONTS, ROWS, COLS = 4, 16, 4
AXES = ("front", "row", "col")
HIGHEST = lax.Precision.HIGHEST
MIB = 2**20


def permute(x, route):
    def flat(f, r, c):
        return (f * ROWS + r) * COLS + c

    pairs = []
    for f in range(FRONTS):
        for r in range(ROWS):
            for c in range(COLS):
                target = route(f, r, c)
                if target is not None:
                    pairs.append((flat(f, r, c), flat(*target)))
    return lax.ppermute(x, AXES, pairs)


def dot(a, b, ca, cb):
    return lax.dot_general(
        a, b, (((ca,), (cb,)), ((), ())), precision=HIGHEST, preferred_element_type=jnp.float32
    )


def vmem():
    return pl.BlockSpec(memory_space=pltpu.VMEM)


def smem():
    return pl.BlockSpec(memory_space=pltpu.SMEM)


def place(dst, col_off, bmap, run, rows, cols, tile):
    for row_id, row_part in rows:
        t = bmap[0, row_id]
        for col_id, fetch in cols:
            u = bmap[0, col_id]

            @pl.when((t // 4 == run) & (u // 4 == tile))
            def _():
                at_r = pl.ds(pl.multiple_of((t % 4) * BLOCK, BLOCK), BLOCK)
                at_c = pl.ds(pl.multiple_of(col_off + (u % 4) * BLOCK, BLOCK), BLOCK)
                dst[at_r, at_c] = dst[at_r, at_c] + fetch(row_part)


def panel_kernel(bmap, order, front, ea, eb, ed, ee, out, packed):
    r = lax.axis_index("row")
    out[...] = front[...]

    def left(part):
        return ea[...] if part == 0 else eb[(part - 1) * BLOCK : part * BLOCK, :]

    def right(which):
        at = slice(which * BLOCK, (which + 1) * BLOCK)

        def fetch(part):
            return ed[:, at] if part == 0 else ee[(part - 1) * BLOCK : part * BLOCK, at]

        return fetch

    rows = [(2 * r, 0), ((2 * r + 30) % 32, 1), ((2 * r + 31) % 32, 2)]
    cols = [(0, left), (30, right(0)), (31, right(1))]
    place(out, 0, bmap, r, rows, cols, 0)
    index = r * 512 + lax.broadcasted_iota(jnp.int32, out.shape, 0)
    out[...] = jnp.where(index < order[0], out[...], 0.0)
    spot = 0
    for i in range(4):
        for j in range(i + 1):
            packed[spot : spot + BLOCK, :] = out[
                i * BLOCK : (i + 1) * BLOCK, j * BLOCK : (j + 1) * BLOCK
            ]
            spot += BLOCK


def panel_call(bmap, order, front, *pieces):
    return pl.pallas_call(
        panel_kernel,
        grid=(1,),
        in_specs=[smem(), smem(), pl.BlockSpec((512, 512), lambda i: (0, 0))] + [vmem()] * 4,
        out_specs=[vmem(), vmem()],
        out_shape=[
            jax.ShapeDtypeStruct((512, 512), jnp.float32),
            jax.ShapeDtypeStruct((1280, 128), jnp.float32),
        ],
        compiler_params=pltpu.CompilerParams(vmem_limit_bytes=16 * MIB),
        name="panel",
    )(bmap, order, front, *pieces)


def reciprocal(d):
    r = pl.reciprocal(d, approx=True)
    r = r * (2.0 - d * r)
    return r * (2.0 - d * r)


def sweep(groups):
    lane = lax.broadcasted_iota(jnp.int32, (8, 128), 1)
    sub = lax.broadcasted_iota(jnp.int32, (8, 128), 0)
    w = list(groups)

    def across(v, k):
        return jnp.broadcast_to(v[:, k : k + 1], (8, 128))

    def down(v, k):
        return jnp.broadcast_to(v[k : k + 1, :], (8, 128))

    for g in range(16):
        base = 8 * g
        top = w[g]
        col = [across(top, base + j) for j in range(8)]
        inverse, pivot = [], {}
        for j in range(8):
            inverse.append(reciprocal(down(col[j], j)))
            m = jnp.where(sub > j, col[j] * inverse[j], 0.0)
            row = jnp.where(lane == base + j, 1.0, down(top, j))
            top = jnp.where((lane == base + j) & (sub > j), 0.0, top) - m * row
            for q in range(j + 1, 8):
                pivot[j, q] = down(col[q], j)
                col[q] = col[q] - m * pivot[j, q]
        w[g] = top
        inside = (lane >= base) & (lane < base + 8)
        rows = []
        for j in range(8):
            later = (lane > base + j) & (lane < base + 8)
            rows.append(jnp.where(lane == base + j, 1.0, jnp.where(later, 0.0, down(top, j))))
        for h in range(g + 1, 16):
            c = [across(w[h], base + j) for j in range(8)]
            acc = jnp.where(inside, 0.0, w[h])
            for j in range(8):
                m = c[j] * inverse[j]
                for q in range(j + 1, 8):
                    c[q] = c[q] - m * pivot[j, q]
                acc = acc - m * rows[j]
            w[h] = acc
    return w


def factor_kernel(p0, p1, p2, p3, out, packed, work, low):
    c = lax.axis_index("col")
    part = p0.shape[0]
    for s, p in enumerate((p0, p1, p2, p3)):
        packed[pl.ds(pl.multiple_of(((c + 4 - s) % 4) * part, part), part), :] = p[...]
    spot = 0
    for i in range(4):
        for j in range(i + 1):
            work[i * BLOCK : (i + 1) * BLOCK, j * BLOCK : (j + 1) * BLOCK] = packed[
                spot : spot + BLOCK, :
            ]
            spot += BLOCK
    out[...] = jnp.zeros_like(out)
    ri = lax.broadcasted_iota(jnp.int32, (BLOCK, BLOCK), 0)
    ci = lax.broadcasted_iota(jnp.int32, (BLOCK, BLOCK), 1)

    def step(j, carry):
        off = pl.multiple_of(j * BLOCK, BLOCK)
        groups = [
            work[pl.ds(pl.multiple_of(off + 8 * g, 8), 8), pl.ds(off, BLOCK)] for g in range(16)
        ]
        w = jnp.concatenate(sweep(groups), axis=0)
        scale = lax.rsqrt(jnp.sum(jnp.where(ri == ci, w, 0.0), axis=1, keepdims=True))
        inv = jnp.where(ri > ci, w, jnp.where(ri == ci, 1.0, 0.0)) * scale
        out[pl.ds(off, BLOCK), pl.ds(off, BLOCK)] = inv
        for jj in range(4):
            lo, hi = jj * BLOCK, (jj + 1) * BLOCK

            @pl.when(j == jj)
            def _():
                if jj < 3:
                    below = dot(work[hi:, lo:hi], inv, 1, 1)
                    work[hi:, hi:] = work[hi:, hi:] - dot(below, below, 1, 1)
                    low[hi:, lo:hi] = below
                if jj > 0:
                    out[lo:hi, :lo] = -dot(inv, dot(low[lo:hi, :lo], out[:lo, :lo], 1, 0), 1, 0)

        return carry

    lax.fori_loop(0, 4, step, 0)


def factor_call(*pieces):
    return pl.pallas_call(
        factor_kernel,
        in_specs=[vmem()] * 4,
        out_specs=vmem(),
        out_shape=jax.ShapeDtypeStruct((512, 512), jnp.float32),
        scratch_shapes=[
            pltpu.VMEM((1280, 128), jnp.float32),
            pltpu.VMEM((512, 512), jnp.float32),
            pltpu.VMEM((512, 512), jnp.float32),
        ],
        compiler_params=pltpu.CompilerParams(vmem_limit_bytes=16 * MIB),
        name="factor",
    )(*pieces)


def update_kernel(
    bmap, order, front, own, prev, edge, a0, a1, a2, a3, linv, a_col, x_out, s_out, a_row, z
):
    r = lax.axis_index("row")
    c = lax.axis_index("col")
    j = pl.program_id(0)

    @pl.when(j == 0)
    def _():
        for s, p in enumerate((a0, a1, a2, a3)):
            at = pl.ds(pl.multiple_of(((c + 4 - s) % 4) * BLOCK, BLOCK), BLOCK)
            a_row[at, :] = p[...]
        x = dot(a_row[...], linv[...], 1, 1)
        x_out[...] = x
        z[...] = dot(x, linv[...], 1, 0)

    s_out[...] = front[...]
    rows = [(2 * r, 0), ((2 * r + 30) % 32, 1), ((2 * r + 31) % 32, 2)]

    def main(k):
        at = slice(k * BLOCK, (k + 1) * BLOCK)

        def fetch(part):
            return own[:BLOCK, at] if part == 0 else prev[(part - 1) * BLOCK : part * BLOCK, at]

        return fetch

    def side(k):
        at = slice(k * BLOCK, (k + 1) * BLOCK)
        return lambda part: edge[part * BLOCK : (part + 1) * BLOCK, at]

    for t in range(4):

        @pl.when(j == t)
        def _():
            first = (8 * c + 2 * t + 30) % 32
            second = (8 * c + 2 * t + 31) % 32
            if t == 0:
                cols = [(first, side(0)), (second, side(1))]
            else:
                cols = [(first, main(2 * t - 2)), (second, main(2 * t - 1))]
            cols.append((8 * c + 2 * t, main(2 * t)))
            place(s_out, 0, bmap, r, rows, cols, 4 * c + t)

    row = r * 512 + lax.broadcasted_iota(jnp.int32, (512, 1), 0)
    col = (4 * c + j) * 512 + lax.broadcasted_iota(jnp.int32, (1, 512), 1)
    keep = (row >= PANEL) & (row < order[0]) & (col >= PANEL) & (col < order[0])
    s_out[...] = jnp.where(keep, s_out[...] - dot(z[...], a_col[...], 1, 1), 0.0)


def update_call(bmap, order, front, own, prev, edge, a_parts, linv, a_col):
    return pl.pallas_call(
        update_kernel,
        grid=(4,),
        in_specs=[smem(), smem(), pl.BlockSpec((512, 512), lambda j: (0, j))]
        + [vmem()] * 8
        + [pl.BlockSpec((512, 512), lambda j: (j, 0))],
        out_specs=[
            pl.BlockSpec((512, 512), lambda j: (0, 0)),
            pl.BlockSpec((512, 512), lambda j: (0, j)),
        ],
        out_shape=[
            jax.ShapeDtypeStruct((512, 512), jnp.float32),
            jax.ShapeDtypeStruct((512, 2048), jnp.float32),
        ],
        scratch_shapes=[
            pltpu.VMEM((512, 512), jnp.float32),
            pltpu.VMEM((512, 512), jnp.float32),
        ],
        compiler_params=pltpu.CompilerParams(vmem_limit_bytes=40 * MIB),
        name="update",
    )(bmap, order, front, own, prev, edge, *a_parts, linv, a_col)


def total(first, *rest):
    for x in rest:
        first = first + x
    return first


def body(front_matrix, child_update, bmap, order):
    front = front_matrix[0]
    child = child_update[0]
    c = lax.axis_index("col")

    ea = permute(child[:128, :128], lambda f, r, c: (f ^ 1, r, 0) if c == 0 else None)
    eb = permute(child[:, :128], lambda f, r, c: (f ^ 1, (r + 1) % ROWS, 0) if c == 0 else None)
    ed = permute(child[:128, 768:], lambda f, r, c: (f ^ 1, r, 0) if c == 3 else None)
    ee = permute(child[:, 768:], lambda f, r, c: (f ^ 1, (r + 1) % ROWS, 0) if c == 3 else None)
    panel, packed = panel_call(bmap, order, front, ea, eb, ed, ee)

    def share(x, rows):
        parts = [x[q * rows : (q + 1) * rows] for q in range(4)]
        return parts

    quarter = share(packed, 320)
    got = [
        permute(quarter[q], lambda f, r, c, q=q: (f, 0, q) if r == 0 and c == 0 else None)
        for q in (1, 2, 3)
    ]
    d = jnp.where(c == 0, quarter[0], total(*got))
    d1 = permute(d, lambda f, r, c: (f, 6, c) if r == 0 else None)
    d2 = permute(d, lambda f, r, c: (f, 12, c) if r == 0 else None)
    here = lax.axis_index("row") == 0
    d = jnp.where(here, d, d1 + d2)
    d1 = permute(d, lambda f, r, c: (f, (r + 2) % ROWS, c) if r in (0, 6, 12) else None)
    d2 = permute(d, lambda f, r, c: (f, r - 2, c) if r in (6, 12) else None)
    row = lax.axis_index("row")
    d = jnp.where((row == 0) | (row == 6) | (row == 12), d, d1 + d2)
    d1 = permute(d, lambda f, r, c: (f, r + 1, c) if r % 2 == 0 else None)
    d = jnp.where(row % 2 == 0, d, d1)

    quarter = share(panel, 128)
    got = [
        permute(quarter[q], lambda f, r, c, q=q: (f, r, q) if c == 0 else None) for q in (1, 2, 3)
    ]
    mine = jnp.where(c == 0, quarter[0], total(*got))
    got = [
        permute(
            quarter[q], lambda f, r, c, q=q: (f, 4 * (r % 4) + q, r // 4) if c == 0 else None
        )
        for q in range(4)
    ]
    a_col = lax.all_gather(total(*got), "row", axis=0, tiled=True)

    d_parts = [d] + [permute(d, lambda f, r, c, s=s: (f, r, (c + s) % COLS)) for s in (1, 2, 3)]
    a_parts = [mine] + [
        permute(mine, lambda f, r, c, s=s: (f, r, (c + s) % COLS)) for s in (1, 2, 3)
    ]

    own = permute(child, lambda f, r, c: (f ^ 1, r, c))
    prev = permute(own, lambda f, r, c: (f, (r + 1) % ROWS, c))
    edge = jnp.concatenate([own[:128, 768:], prev[:, 768:]], axis=0)
    edge = permute(edge, lambda f, r, c: (f, r, (c + 1) % COLS))

    linv = factor_call(*d_parts)
    x, s = update_call(bmap, order, front, own, prev, edge, a_parts, linv, a_col)
    return x[None], s[None]


def solution(mesh):
    return jax.shard_map(
        body,
        mesh=mesh,
        in_specs=(P("front", "row", "col"), P("front", "row", "col"), P("front", None), P("front")),
        out_specs=(P("front", "row", None), P("front", "row", "col")),
        check_vma=False,
    )
```

```python
import jax
import jax.numpy as jnp
from jax import lax
from jax.experimental import pallas as pl
from jax.experimental.pallas import tpu as pltpu
from jax.sharding import PartitionSpec as P

BLOCK = 128
PANEL = 512
FRONTS, ROWS, COLS = 4, 16, 4
AXES = ("front", "row", "col")
HIGHEST = lax.Precision.HIGHEST
MIB = 2**20


def permute(x, route):
    def flat(f, r, c):
        return (f * ROWS + r) * COLS + c

    pairs = []
    for f in range(FRONTS):
        for r in range(ROWS):
            for c in range(COLS):
                target = route(f, r, c)
                if target is not None:
                    pairs.append((flat(f, r, c), flat(*target)))
    return lax.ppermute(x, AXES, pairs)


def dot(a, b, ca, cb):
    return lax.dot_general(
        a, b, (((ca,), (cb,)), ((), ())), precision=HIGHEST, preferred_element_type=jnp.float32
    )


def smem():
    return pl.BlockSpec(memory_space=pltpu.SMEM)


def hbm():
    return pl.BlockSpec(memory_space=pltpu.HBM)


def whole(shape):
    return pl.BlockSpec(shape, lambda i: (0,) * len(shape))


def place(dst, col_off, bmap, run, rows, cols, tile):
    for row_id, row_part in rows:
        t = bmap[0, row_id]
        for col_id, fetch in cols:
            u = bmap[0, col_id]

            @pl.when((t // 4 == run) & (u // 4 == tile))
            def _():
                at_r = pl.ds(pl.multiple_of((t % 4) * BLOCK, BLOCK), BLOCK)
                at_c = pl.ds(pl.multiple_of(col_off + (u % 4) * BLOCK, BLOCK), BLOCK)
                dst[at_r, at_c] = dst[at_r, at_c] + fetch(row_part)


def pack_kernel(left, right, block, ea, eb, ed, ee, top, bottom):
    top[...] = block[:BLOCK, :]
    bottom[...] = block[BLOCK:, :]
    ea[...] = left[:BLOCK, :]
    eb[...] = left[...]
    ed[...] = right[:BLOCK, :]
    ee[...] = right[...]


def pack_call(child):
    shapes = [(128, 128), (256, 128), (128, 256), (256, 256), (128, 1024), (128, 1024)]
    return pl.pallas_call(
        pack_kernel,
        grid=(1,),
        in_specs=[
            pl.BlockSpec((256, 128), lambda i: (0, 0)),
            pl.BlockSpec((256, 256), lambda i: (0, 3)),
            pl.BlockSpec((256, 1024), lambda i: (0, 0)),
        ],
        out_specs=[whole(x) for x in shapes],
        out_shape=[jax.ShapeDtypeStruct(x, jnp.float32) for x in shapes],
        name="pack",
    )(child, child, child)


def panel_kernel(bmap, order, front, ea, eb, ed, ee, q0, q1, q2, q3, work):
    r = lax.axis_index("row")
    work[...] = front[...]

    def left(part):
        return ea[...] if part == 0 else eb[(part - 1) * BLOCK : part * BLOCK, :]

    def right(which):
        at = slice(which * BLOCK, (which + 1) * BLOCK)

        def fetch(part):
            return ed[:, at] if part == 0 else ee[(part - 1) * BLOCK : part * BLOCK, at]

        return fetch

    rows = [(2 * r, 0), ((2 * r + 30) % 32, 1), ((2 * r + 31) % 32, 2)]
    cols = [(0, left), (30, right(0)), (31, right(1))]
    place(work, 0, bmap, r, rows, cols, 0)
    for q, out in enumerate((q0, q1, q2, q3)):
        index = r * 512 + q * BLOCK + lax.broadcasted_iota(jnp.int32, out.shape, 0)
        out[...] = jnp.where(index < order[0], work[q * BLOCK : (q + 1) * BLOCK, :], 0.0)


def panel_call(bmap, order, front, *pieces):
    return pl.pallas_call(
        panel_kernel,
        grid=(1,),
        in_specs=[smem(), smem(), whole((512, 512))] + [whole(p.shape) for p in pieces],
        out_specs=[whole((128, 512))] * 4,
        out_shape=[jax.ShapeDtypeStruct((128, 512), jnp.float32)] * 4,
        scratch_shapes=[pltpu.VMEM((512, 512), jnp.float32)],
        compiler_params=pltpu.CompilerParams(vmem_limit_bytes=16 * MIB),
        name="panel",
    )(bmap, order, front, *pieces)


def reciprocal(d):
    r = pl.reciprocal(d, approx=True)
    r = r * (2.0 - d * r)
    return r * (2.0 - d * r)


def sweep(groups):
    lane = lax.broadcasted_iota(jnp.int32, (8, 128), 1)
    sub = lax.broadcasted_iota(jnp.int32, (8, 128), 0)
    w = list(groups)

    def across(v, k):
        return jnp.broadcast_to(v[:, k : k + 1], (8, 128))

    def down(v, k):
        return jnp.broadcast_to(v[k : k + 1, :], (8, 128))

    for g in range(16):
        base = 8 * g
        top = w[g]
        col = [across(top, base + j) for j in range(8)]
        inverse, pivot = [], {}
        for j in range(8):
            inverse.append(reciprocal(down(col[j], j)))
            m = jnp.where(sub > j, col[j] * inverse[j], 0.0)
            row = jnp.where(lane == base + j, 1.0, down(top, j))
            top = jnp.where((lane == base + j) & (sub > j), 0.0, top) - m * row
            for q in range(j + 1, 8):
                pivot[j, q] = down(col[q], j)
                col[q] = col[q] - m * pivot[j, q]
        w[g] = top
        inside = (lane >= base) & (lane < base + 8)
        rows = []
        for j in range(8):
            later = (lane > base + j) & (lane < base + 8)
            rows.append(jnp.where(lane == base + j, 1.0, jnp.where(later, 0.0, down(top, j))))
        for h in range(g + 1, 16):
            c = [across(w[h], base + j) for j in range(8)]
            acc = jnp.where(inside, 0.0, w[h])
            for j in range(8):
                m = c[j] * inverse[j]
                for q in range(j + 1, 8):
                    c[q] = c[q] - m * pivot[j, q]
                acc = acc - m * rows[j]
            w[h] = acc
    return w


def gather_rows(dst, parts):
    c = lax.axis_index("col")
    rows = dst.shape[0] // 4
    for s, p in enumerate(parts):
        at = pl.ds(pl.multiple_of(((c + 4 - s) % 4) * rows, rows), rows)
        dst[at, :] = p[...]


def invert(work, out, low):
    ri = lax.broadcasted_iota(jnp.int32, (BLOCK, BLOCK), 0)
    ci = lax.broadcasted_iota(jnp.int32, (BLOCK, BLOCK), 1)

    def step(j, carry):
        off = pl.multiple_of(j * BLOCK, BLOCK)
        groups = [
            work[pl.ds(pl.multiple_of(off + 8 * g, 8), 8), pl.ds(off, BLOCK)] for g in range(16)
        ]
        w = jnp.concatenate(sweep(groups), axis=0)
        scale = lax.rsqrt(jnp.sum(jnp.where(ri == ci, w, 0.0), axis=1, keepdims=True))
        inv = jnp.where(ri > ci, w, jnp.where(ri == ci, 1.0, 0.0)) * scale
        out[pl.ds(off, BLOCK), pl.ds(off, BLOCK)] = inv

        @pl.when(j == 0)
        def _():
            below = dot(work[BLOCK:, :BLOCK], inv, 1, 1)
            work[BLOCK:, BLOCK:] = work[BLOCK:, BLOCK:] - dot(below, below, 1, 1)
            low[...] = below

        @pl.when(j == 1)
        def _():
            out[BLOCK:, :BLOCK] = -dot(inv, dot(low[...], out[:BLOCK, :BLOCK], 1, 0), 1, 0)
            out[:BLOCK, BLOCK:] = jnp.zeros((BLOCK, BLOCK), jnp.float32)

        return carry

    lax.fori_loop(0, 2, step, 0)


HALF = (256, 256)


def first_kernel(q0, q1, q2, q3, inv, below, rest, work, low):
    work[:BLOCK, :] = q0[:, :256]
    work[BLOCK:, :] = q1[:, :256]
    invert(work, inv, low)
    x = dot(jnp.concatenate([q2[:, :256], q3[:, :256]], axis=0), inv[...], 1, 1)
    below[...] = x
    rest[...] = jnp.concatenate([q2[:, 256:], q3[:, 256:]], axis=0) - dot(x, x, 1, 1)


def first_call(quarter):
    return pl.pallas_call(
        first_kernel,
        grid=(1,),
        in_specs=[whole((128, 512))] * 4,
        out_specs=[whole(HALF)] * 3,
        out_shape=[jax.ShapeDtypeStruct(HALF, jnp.float32)] * 3,
        scratch_shapes=[pltpu.VMEM(HALF, jnp.float32), pltpu.VMEM((BLOCK, BLOCK), jnp.float32)],
        compiler_params=pltpu.CompilerParams(vmem_limit_bytes=16 * MIB),
        cost_estimate=pl.CostEstimate(flops=10**10, bytes_accessed=4 * MIB, transcendentals=0),
        name="first",
    )(*quarter)


def second_kernel(inv, below, rest, k0, k1, k2, k3, work, out, low, packed):
    work[...] = rest[...]
    invert(work, out, low)
    corner = -dot(out[...], dot(below[...], inv[...], 1, 0), 1, 0)
    spots = [(inv, 0, 0), (inv, 1, 0), (inv, 1, 1), (out, 0, 0), (out, 1, 0), (out, 1, 1)]
    for k, (src, i, j) in enumerate(spots):
        packed[k * BLOCK : (k + 1) * BLOCK, :] = src[
            i * BLOCK : (i + 1) * BLOCK, j * BLOCK : (j + 1) * BLOCK
        ]
    packed[768:1024, :] = corner[:, :BLOCK]
    packed[1024:, :] = corner[:, BLOCK:]
    for q, k in enumerate((k0, k1, k2, k3)):
        k[...] = packed[q * 320 : (q + 1) * 320, :]


def unpack(linv, packed):
    linv[...] = jnp.zeros_like(linv)
    for k, (i, j) in enumerate(((0, 0), (1, 0), (1, 1), (2, 2), (3, 2), (3, 3))):
        linv[i * BLOCK : (i + 1) * BLOCK, j * BLOCK : (j + 1) * BLOCK] = packed[
            k * BLOCK : (k + 1) * BLOCK, :
        ]
    linv[256:, :BLOCK] = packed[768:1024, :]
    linv[256:, BLOCK:256] = packed[1024:, :]


def second_call(inv, below, rest):
    part = (320, 128)
    return pl.pallas_call(
        second_kernel,
        grid=(1,),
        in_specs=[whole(HALF)] * 3,
        out_specs=[whole(part)] * 4,
        out_shape=[jax.ShapeDtypeStruct(part, jnp.float32)] * 4,
        scratch_shapes=[
            pltpu.VMEM(HALF, jnp.float32),
            pltpu.VMEM(HALF, jnp.float32),
            pltpu.VMEM((BLOCK, BLOCK), jnp.float32),
            pltpu.VMEM((1280, 128), jnp.float32),
        ],
        compiler_params=pltpu.CompilerParams(vmem_limit_bytes=16 * MIB),
        cost_estimate=pl.CostEstimate(flops=10**10, bytes_accessed=4 * MIB, transcendentals=0),
        name="second",
    )(inv, below, rest)


def halves(x):
    high = x.astype(jnp.bfloat16)
    return high, (x - high.astype(jnp.float32)).astype(jnp.bfloat16)


def dot3(a_high, a_low, b_high, b_low):
    def part(x, y):
        return lax.dot_general(
            x, y, (((1,), (1,)), ((), ())), preferred_element_type=jnp.float32
        )

    return part(a_high, b_high) + (part(a_high, b_low) + part(a_low, b_high))


def update_kernel(
    bmap, order, l0, l1, l2, l3, a0, a1, a2, a3, front, own, prev0, prev1, edge0, edge1, a_col,
    x_out, s_out, packed, linv, a_row, x_buf, z_high, z_low, child, tiles, cols, front_sem, col_sem, child_sem, x_sem, s_sem,
):
    r = lax.axis_index("row")
    c = lax.axis_index("col")
    wide = child.shape[1]

    def columns(t):
        return pl.ds(pl.multiple_of(t * 512, 512), 512)

    def front_copy(t):
        return pltpu.make_async_copy(front.at[:, columns(t)], tiles.at[t], front_sem.at[t])

    def col_copy(t):
        return pltpu.make_async_copy(a_col.at[columns(t), :], cols.at[t], col_sem.at[t])

    def out_copy(t):
        return pltpu.make_async_copy(tiles.at[t], s_out.at[:, columns(t)], s_sem.at[t])

    upper, rest = pl.ds(0, BLOCK), pl.ds(BLOCK, 2 * BLOCK)
    middle, lower = pl.ds(BLOCK, BLOCK), pl.ds(2 * BLOCK, BLOCK)
    left, right = pl.ds(0, 2 * BLOCK), pl.ds(2 * BLOCK, wide - 2 * BLOCK)
    child_copies = [
        pltpu.make_async_copy(src, child.at[at], child_sem.at[k])
        for k, (src, at) in enumerate(
            [
                (own, (upper, right)),
                (prev0, (middle, right)),
                (prev1, (lower, right)),
                (edge0, (upper, left)),
                (edge1, (rest, left)),
            ]
        )
    ]
    front_copy(0).start()
    for copy in child_copies:
        copy.start()
    col_copy(0).start()
    for t in range(1, 4):
        front_copy(t).start()
        col_copy(t).start()

    gather_rows(packed, (l0, l1, l2, l3))
    unpack(linv, packed)
    gather_rows(a_row, (a0, a1, a2, a3))
    x = dot(a_row[...], linv[...], 1, 1)
    x_buf[...] = x
    x_copy = pltpu.make_async_copy(x_buf, x_out, x_sem)
    x_copy.start()
    high, low = halves(dot(x, linv[...], 1, 0))
    z_high[...] = high
    z_low[...] = low
    for copy in child_copies:
        copy.wait()

    rows = [(2 * r, 0), ((2 * r + 30) % 32, 1), ((2 * r + 31) % 32, 2)]
    row = r * 512 + lax.broadcasted_iota(jnp.int32, (512, 1), 0)

    def step(t, carry):
        front_copy(t).wait()
        tile = tiles.at[t]

        def block(k):
            at = pl.ds(pl.multiple_of((2 * t + k) * BLOCK, BLOCK), BLOCK)
            return lambda part: child[part * BLOCK : (part + 1) * BLOCK, at]

        ids = [((8 * c + 2 * t + 30 + k) % 32, block(k)) for k in range(3)]
        place(tile, 0, bmap, r, rows, ids, 4 * c + t)
        col_copy(t).wait()
        col = (4 * c + t) * 512 + lax.broadcasted_iota(jnp.int32, (1, 512), 1)
        keep = (row >= PANEL) & (row < order[0]) & (col >= PANEL) & (col < order[0])
        product = dot3(z_high[...], z_low[...], *halves(cols[t]))
        tile[...] = jnp.where(keep, tile[...] - product, 0.0)
        out_copy(t).start()
        return carry

    lax.fori_loop(0, 4, step, 0)
    x_copy.wait()
    for t in range(4):
        out_copy(t).wait()


def update_call(bmap, order, l_parts, a_parts, front, own, prev0, prev1, edge0, edge1, a_col):
    square = (512, 512)
    return pl.pallas_call(
        update_kernel,
        grid=(1,),
        in_specs=[smem(), smem()]
        + [whole((320, 128))] * 4
        + [whole((128, 512))] * 4
        + [hbm()] * 7,
        out_specs=[hbm(), hbm()],
        out_shape=[
            jax.ShapeDtypeStruct(square, jnp.float32),
            jax.ShapeDtypeStruct((512, 2048), jnp.float32),
        ],
        scratch_shapes=[
            pltpu.VMEM((1280, 128), jnp.float32),
            pltpu.VMEM(square, jnp.float32),
            pltpu.VMEM(square, jnp.float32),
            pltpu.VMEM(square, jnp.float32),
            pltpu.VMEM(square, jnp.bfloat16),
            pltpu.VMEM(square, jnp.bfloat16),
            pltpu.VMEM((384, 1280), jnp.float32),
            pltpu.VMEM((4, 512, 512), jnp.float32),
            pltpu.VMEM((4, 512, 512), jnp.float32),
            pltpu.SemaphoreType.DMA((4,)),
            pltpu.SemaphoreType.DMA((4,)),
            pltpu.SemaphoreType.DMA((5,)),
            pltpu.SemaphoreType.DMA,
            pltpu.SemaphoreType.DMA((4,)),
        ],
        compiler_params=pltpu.CompilerParams(vmem_limit_bytes=60 * MIB),
        name="update",
    )(bmap, order, *l_parts, *a_parts, front, own, prev0, prev1, edge0, edge1, a_col)


def after(x, *earlier):
    return lax.optimization_barrier((x, *earlier))[0]


def body(front_matrix, child_update, bmap, order):
    front = front_matrix[0]
    child = child_update[0]
    row = lax.axis_index("row")
    c = lax.axis_index("col")

    ea, eb, e0, e1, top, bottom = pack_call(child)
    ee = permute(e1, lambda f, r, c: (f ^ 1, (r + 1) % ROWS, 0) if c == 3 else None)
    ed = permute(e0, lambda f, r, c: (f ^ 1, r, 0) if c == 3 else None)
    eb = permute(eb, lambda f, r, c: (f ^ 1, (r + 1) % ROWS, 0) if c == 0 else None)
    ea = permute(ea, lambda f, r, c: (f ^ 1, r, 0) if c == 0 else None)
    quarter = panel_call(bmap, order, front[:, :PANEL], ea, eb, ed, ee)

    def across(x):
        return permute(x, lambda f, r, c: (f ^ 1, r, c))

    top, bottom, e0, e1, _ = lax.optimization_barrier((top, bottom, e0, e1, quarter[0]))
    own = across(top)
    prev1 = permute(bottom, lambda f, r, c: (f, (r + 1) % ROWS, c))

    got = [
        permute(quarter[q], lambda f, r, c, q=q: (f, r, q) if c == 0 else None) for q in (1, 2, 3)
    ]

    half = first_call(quarter)
    *got, own, prev1, e0, e1, _ = lax.optimization_barrier((*got, own, prev1, e0, e1, half[0]))
    prev1 = across(prev1)
    prev0 = permute(own, lambda f, r, c: (f, (r + 1) % ROWS, c))
    edge0 = permute(e0, lambda f, r, c: (f, r, (c + 1) % COLS))
    edge1 = permute(e1, lambda f, r, c: (f, (r + 1) % ROWS, (c + 1) % COLS))
    mine = jnp.where(c == 0, quarter[0], got[0] + got[1] + got[2])

    piece = permute(mine, lambda f, r, c: (f, 4 * (r % 4) + c, r // 4))

    *half, _, _ = lax.optimization_barrier((*half, mine, own))
    part = second_call(*half)
    piece, prev0, prev1, edge0, edge1, *part = lax.optimization_barrier(
        (piece, prev0, prev1, edge0, edge1, *part)
    )
    edge0, edge1 = across(edge0), across(edge1)
    a_col = lax.all_gather(piece, "row", axis=0, tiled=True)

    got = [
        permute(part[q], lambda f, r, c, q=q: (f, 0, q) if r == 0 and c == 0 else None)
        for q in (1, 2, 3)
    ]
    d = jnp.where(c == 0, part[0], got[0] + got[1] + got[2])

    m = after(mine, part[0])
    a_parts = [permute(m, lambda f, r, c, s=s: (f, r, (c + s) % COLS)) for s in (1, 2, 3)]

    d1 = permute(d, lambda f, r, c: (f, 6, c) if r == 0 else None)
    d2 = permute(d, lambda f, r, c: (f, 12, c) if r == 0 else None)
    d = jnp.where(row == 0, d, d1 + d2)
    d, *a_parts = lax.optimization_barrier((d, *a_parts))
    a_parts = [mine, *a_parts]
    d1 = permute(d, lambda f, r, c: (f, (r + 2) % ROWS, c) if r in (0, 6, 12) else None)
    d2 = permute(d, lambda f, r, c: (f, r - 2, c) if r in (6, 12) else None)
    d = jnp.where((row == 0) | (row == 6) | (row == 12), d, d1 + d2)
    d1 = permute(d, lambda f, r, c: (f, r + 1, c) if r % 2 == 0 else None)
    d = jnp.where(row % 2 == 0, d, d1)
    l_parts = [d] + [permute(d, lambda f, r, c, s=s: (f, r, (c + s) % COLS)) for s in (1, 2, 3)]

    x, s = update_call(bmap, order, l_parts, a_parts, front, own, prev0, prev1, edge0, edge1, a_col)
    return x[None], s[None]


def solution(mesh):
    return jax.shard_map(
        body,
        mesh=mesh,
        in_specs=(P("front", "row", "col"), P("front", "row", "col"), P("front", None), P("front")),
        out_specs=(P("front", "row", None), P("front", "row", "col")),
        check_vma=False,
    )
```

```python
import jax
import jax.numpy as jnp
from jax import lax
from jax.experimental import pallas as pl
from jax.experimental.pallas import tpu as pltpu
from jax.sharding import PartitionSpec as P

BLOCK = 128
PANEL = 512
FRONTS, ROWS, COLS = 4, 16, 4
AXES = ("front", "row", "col")
HIGHEST = lax.Precision.HIGHEST
MIB = 2**20


def permute(x, route):
    def flat(f, r, c):
        return (f * ROWS + r) * COLS + c

    pairs = []
    for f in range(FRONTS):
        for r in range(ROWS):
            for c in range(COLS):
                target = route(f, r, c)
                if target is not None:
                    pairs.append((flat(f, r, c), flat(*target)))
    return lax.ppermute(x, AXES, pairs)


def dot(a, b, ca, cb):
    return lax.dot_general(
        a, b, (((ca,), (cb,)), ((), ())), precision=HIGHEST, preferred_element_type=jnp.float32
    )


def smem():
    return pl.BlockSpec(memory_space=pltpu.SMEM)


def hbm():
    return pl.BlockSpec(memory_space=pltpu.HBM)


def whole(shape):
    return pl.BlockSpec(shape, lambda i: (0,) * len(shape))


def place(dst, col_off, bmap, run, rows, cols, tile):
    for row_id, row_part in rows:
        t = bmap[0, row_id]
        for col_id, fetch in cols:
            u = bmap[0, col_id]

            @pl.when((t // 4 == run) & (u // 4 == tile))
            def _():
                at_r = pl.ds(pl.multiple_of((t % 4) * BLOCK, BLOCK), BLOCK)
                at_c = pl.ds(pl.multiple_of(col_off + (u % 4) * BLOCK, BLOCK), BLOCK)
                dst[at_r, at_c] = dst[at_r, at_c] + fetch(row_part)


def pack_kernel(left, right, block, ea, eb, ed, ee, top, bottom):
    top[...] = block[:BLOCK, :]
    bottom[...] = block[BLOCK:, :]
    ea[...] = left[:BLOCK, :]
    eb[...] = left[...]
    ed[...] = right[:BLOCK, :]
    ee[...] = right[...]


def pack_call(child):
    shapes = [(128, 128), (256, 128), (128, 256), (256, 256), (128, 1024), (128, 1024)]
    return pl.pallas_call(
        pack_kernel,
        grid=(1,),
        in_specs=[
            pl.BlockSpec((256, 128), lambda i: (0, 0)),
            pl.BlockSpec((256, 256), lambda i: (0, 3)),
            pl.BlockSpec((256, 1024), lambda i: (0, 0)),
        ],
        out_specs=[whole(x) for x in shapes],
        out_shape=[jax.ShapeDtypeStruct(x, jnp.float32) for x in shapes],
        name="pack",
    )(child, child, child)


def panel_kernel(bmap, order, front, ea, eb, ed, ee, q0, q1, q2, q3, work):
    r = lax.axis_index("row")
    work[...] = front[...]

    def left(part):
        return ea[...] if part == 0 else eb[(part - 1) * BLOCK : part * BLOCK, :]

    def right(which):
        at = slice(which * BLOCK, (which + 1) * BLOCK)

        def fetch(part):
            return ed[:, at] if part == 0 else ee[(part - 1) * BLOCK : part * BLOCK, at]

        return fetch

    rows = [(2 * r, 0), ((2 * r + 30) % 32, 1), ((2 * r + 31) % 32, 2)]
    cols = [(0, left), (30, right(0)), (31, right(1))]
    place(work, 0, bmap, r, rows, cols, 0)
    for q, out in enumerate((q0, q1, q2, q3)):
        index = r * 512 + q * BLOCK + lax.broadcasted_iota(jnp.int32, out.shape, 0)
        out[...] = jnp.where(index < order[0], work[q * BLOCK : (q + 1) * BLOCK, :], 0.0)


def panel_call(bmap, order, front, *pieces):
    return pl.pallas_call(
        panel_kernel,
        grid=(1,),
        in_specs=[smem(), smem(), whole((512, 512))] + [whole(p.shape) for p in pieces],
        out_specs=[whole((128, 512))] * 4,
        out_shape=[jax.ShapeDtypeStruct((128, 512), jnp.float32)] * 4,
        scratch_shapes=[pltpu.VMEM((512, 512), jnp.float32)],
        compiler_params=pltpu.CompilerParams(vmem_limit_bytes=16 * MIB),
        name="panel",
    )(bmap, order, front, *pieces)


def reciprocal(d):
    r = pl.reciprocal(d, approx=True)
    r = r * (2.0 - d * r)
    return r * (2.0 - d * r)


def sweep(groups):
    lane = lax.broadcasted_iota(jnp.int32, (8, 128), 1)
    sub = lax.broadcasted_iota(jnp.int32, (8, 128), 0)
    w = list(groups)

    def across(v, k):
        return jnp.broadcast_to(v[:, k : k + 1], (8, 128))

    def down(v, k):
        return jnp.broadcast_to(v[k : k + 1, :], (8, 128))

    for g in range(16):
        base = 8 * g
        top = w[g]
        col = [across(top, base + j) for j in range(8)]
        inverse, pivot = [], {}
        for j in range(8):
            inverse.append(reciprocal(down(col[j], j)))
            m = jnp.where(sub > j, col[j] * inverse[j], 0.0)
            row = jnp.where(lane == base + j, 1.0, down(top, j))
            top = jnp.where((lane == base + j) & (sub > j), 0.0, top) - m * row
            for q in range(j + 1, 8):
                pivot[j, q] = down(col[q], j)
                col[q] = col[q] - m * pivot[j, q]
        w[g] = top
        inside = (lane >= base) & (lane < base + 8)
        rows = []
        for j in range(8):
            later = (lane > base + j) & (lane < base + 8)
            rows.append(jnp.where(lane == base + j, 1.0, jnp.where(later, 0.0, down(top, j))))
        for h in range(g + 1, 16):
            c = [across(w[h], base + j) for j in range(8)]
            acc = jnp.where(inside, 0.0, w[h])
            for j in range(8):
                m = c[j] * inverse[j]
                for q in range(j + 1, 8):
                    c[q] = c[q] - m * pivot[j, q]
                acc = acc - m * rows[j]
            w[h] = acc
    return w


def gather_rows(dst, parts):
    c = lax.axis_index("col")
    rows = dst.shape[0] // 4
    for s, p in enumerate(parts):
        at = pl.ds(pl.multiple_of(((c + 4 - s) % 4) * rows, rows), rows)
        dst[at, :] = p[...]


def invert(work, out, low):
    ri = lax.broadcasted_iota(jnp.int32, (BLOCK, BLOCK), 0)
    ci = lax.broadcasted_iota(jnp.int32, (BLOCK, BLOCK), 1)

    def step(j, carry):
        off = pl.multiple_of(j * BLOCK, BLOCK)
        groups = [
            work[pl.ds(pl.multiple_of(off + 8 * g, 8), 8), pl.ds(off, BLOCK)] for g in range(16)
        ]
        w = jnp.concatenate(sweep(groups), axis=0)
        scale = lax.rsqrt(jnp.sum(jnp.where(ri == ci, w, 0.0), axis=1, keepdims=True))
        inv = jnp.where(ri > ci, w, jnp.where(ri == ci, 1.0, 0.0)) * scale
        out[pl.ds(off, BLOCK), pl.ds(off, BLOCK)] = inv

        @pl.when(j == 0)
        def _():
            below = dot(work[BLOCK:, :BLOCK], inv, 1, 1)
            work[BLOCK:, BLOCK:] = work[BLOCK:, BLOCK:] - dot(below, below, 1, 1)
            low[...] = below

        @pl.when(j == 1)
        def _():
            out[BLOCK:, :BLOCK] = -dot(inv, dot(low[...], out[:BLOCK, :BLOCK], 1, 0), 1, 0)
            out[:BLOCK, BLOCK:] = jnp.zeros((BLOCK, BLOCK), jnp.float32)

        return carry

    lax.fori_loop(0, 2, step, 0)


HALF = (256, 256)


def first_kernel(q0, q1, q2, q3, inv, below, rest, work, low):
    work[:BLOCK, :] = q0[:, :256]
    work[BLOCK:, :] = q1[:, :256]
    invert(work, inv, low)
    x = dot(jnp.concatenate([q2[:, :256], q3[:, :256]], axis=0), inv[...], 1, 1)
    below[...] = x
    rest[...] = jnp.concatenate([q2[:, 256:], q3[:, 256:]], axis=0) - dot(x, x, 1, 1)


def first_call(quarter):
    return pl.pallas_call(
        first_kernel,
        grid=(1,),
        in_specs=[whole((128, 512))] * 4,
        out_specs=[whole(HALF)] * 3,
        out_shape=[jax.ShapeDtypeStruct(HALF, jnp.float32)] * 3,
        scratch_shapes=[pltpu.VMEM(HALF, jnp.float32), pltpu.VMEM((BLOCK, BLOCK), jnp.float32)],
        compiler_params=pltpu.CompilerParams(vmem_limit_bytes=16 * MIB),
        cost_estimate=pl.CostEstimate(flops=10**10, bytes_accessed=4 * MIB, transcendentals=0),
        name="first",
    )(*quarter)


def second_kernel(inv, below, rest, k0, k1, k2, k3, work, out, low, packed):
    work[...] = rest[...]
    invert(work, out, low)
    corner = -dot(out[...], dot(below[...], inv[...], 1, 0), 1, 0)
    spots = [(inv, 0, 0), (inv, 1, 0), (inv, 1, 1), (out, 0, 0), (out, 1, 0), (out, 1, 1)]
    for k, (src, i, j) in enumerate(spots):
        packed[k * BLOCK : (k + 1) * BLOCK, :] = src[
            i * BLOCK : (i + 1) * BLOCK, j * BLOCK : (j + 1) * BLOCK
        ]
    packed[768:1024, :] = corner[:, :BLOCK]
    packed[1024:, :] = corner[:, BLOCK:]
    for q, k in enumerate((k0, k1, k2, k3)):
        k[...] = packed[q * 320 : (q + 1) * 320, :]


def unpack(linv, packed):
    linv[...] = jnp.zeros_like(linv)
    for k, (i, j) in enumerate(((0, 0), (1, 0), (1, 1), (2, 2), (3, 2), (3, 3))):
        linv[i * BLOCK : (i + 1) * BLOCK, j * BLOCK : (j + 1) * BLOCK] = packed[
            k * BLOCK : (k + 1) * BLOCK, :
        ]
    linv[256:, :BLOCK] = packed[768:1024, :]
    linv[256:, BLOCK:256] = packed[1024:, :]


def second_call(inv, below, rest):
    part = (320, 128)
    return pl.pallas_call(
        second_kernel,
        grid=(1,),
        in_specs=[whole(HALF)] * 3,
        out_specs=[whole(part)] * 4,
        out_shape=[jax.ShapeDtypeStruct(part, jnp.float32)] * 4,
        scratch_shapes=[
            pltpu.VMEM(HALF, jnp.float32),
            pltpu.VMEM(HALF, jnp.float32),
            pltpu.VMEM((BLOCK, BLOCK), jnp.float32),
            pltpu.VMEM((1280, 128), jnp.float32),
        ],
        compiler_params=pltpu.CompilerParams(vmem_limit_bytes=16 * MIB),
        cost_estimate=pl.CostEstimate(flops=10**10, bytes_accessed=4 * MIB, transcendentals=0),
        name="second",
    )(inv, below, rest)


def halves(x):
    high = x.astype(jnp.bfloat16)
    return high, (x - high.astype(jnp.float32)).astype(jnp.bfloat16)


def dot3(a_high, a_low, b_high, b_low):
    def part(x, y):
        return lax.dot_general(
            x, y, (((1,), (1,)), ((), ())), preferred_element_type=jnp.float32
        )

    return part(a_high, b_high) + (part(a_high, b_low) + part(a_low, b_high))


def update_kernel(
    bmap, order, l0, l1, l2, l3, a0, a1, a2, a3, front, own, prev0, prev1, edge0, edge1, a_col,
    x_out, s_out, packed, linv, a_row, x_buf, z_high, z_low, child, tiles, cols, front_sem, col_sem, child_sem, x_sem, s_sem,
):
    r = lax.axis_index("row")
    c = lax.axis_index("col")
    wide = child.shape[1]

    def columns(t):
        return pl.ds(pl.multiple_of(t * 512, 512), 512)

    def front_copy(t):
        return pltpu.make_async_copy(front.at[:, columns(t)], tiles.at[t], front_sem.at[t])

    def col_copy(t):
        return pltpu.make_async_copy(a_col.at[columns(t), :], cols.at[t], col_sem.at[t])

    def out_copy(t):
        return pltpu.make_async_copy(tiles.at[t], s_out.at[:, columns(t)], s_sem.at[t])

    upper, rest = pl.ds(0, BLOCK), pl.ds(BLOCK, 2 * BLOCK)
    middle, lower = pl.ds(BLOCK, BLOCK), pl.ds(2 * BLOCK, BLOCK)
    left, right = pl.ds(0, 2 * BLOCK), pl.ds(2 * BLOCK, wide - 2 * BLOCK)
    child_copies = [
        pltpu.make_async_copy(src, child.at[at], child_sem.at[k])
        for k, (src, at) in enumerate(
            [
                (own, (upper, right)),
                (prev0, (middle, right)),
                (prev1, (lower, right)),
                (edge0.at[upper, :], (upper, left)),
                (edge1, (rest, left)),
            ]
        )
    ]
    front_copy(0).start()
    for copy in child_copies:
        copy.start()
    col_copy(0).start()
    for t in range(1, 4):
        front_copy(t).start()
        col_copy(t).start()

    gather_rows(packed, (l0, l1, l2, l3))
    unpack(linv, packed)
    gather_rows(a_row, (a0, a1, a2, a3))
    x = dot(a_row[...], linv[...], 1, 1)
    x_buf[...] = x
    x_copy = pltpu.make_async_copy(x_buf, x_out, x_sem)
    x_copy.start()
    high, low = halves(dot(x, linv[...], 1, 0))
    z_high[...] = high
    z_low[...] = low
    for copy in child_copies:
        copy.wait()

    rows = [(2 * r, 0), ((2 * r + 30) % 32, 1), ((2 * r + 31) % 32, 2)]
    row = r * 512 + lax.broadcasted_iota(jnp.int32, (512, 1), 0)

    def step(t, carry):
        front_copy(t).wait()
        tile = tiles.at[t]

        def block(k):
            at = pl.ds(pl.multiple_of((2 * t + k) * BLOCK, BLOCK), BLOCK)
            return lambda part: child[part * BLOCK : (part + 1) * BLOCK, at]

        ids = [((8 * c + 2 * t + 30 + k) % 32, block(k)) for k in range(3)]
        place(tile, 0, bmap, r, rows, ids, 4 * c + t)
        col_copy(t).wait()
        col = (4 * c + t) * 512 + lax.broadcasted_iota(jnp.int32, (1, 512), 1)
        keep = (row >= PANEL) & (row < order[0]) & (col >= PANEL) & (col < order[0])
        product = dot3(z_high[...], z_low[...], *halves(cols[t]))
        tile[...] = jnp.where(keep, tile[...] - product, 0.0)
        out_copy(t).start()
        return carry

    lax.fori_loop(0, 4, step, 0)
    x_copy.wait()
    for t in range(4):
        out_copy(t).wait()


def update_call(bmap, order, l_parts, a_parts, front, own, prev0, prev1, edge0, edge1, a_col):
    square = (512, 512)
    return pl.pallas_call(
        update_kernel,
        grid=(1,),
        in_specs=[smem(), smem()]
        + [whole((320, 128))] * 4
        + [whole((128, 512))] * 4
        + [hbm()] * 7,
        out_specs=[hbm(), hbm()],
        out_shape=[
            jax.ShapeDtypeStruct(square, jnp.float32),
            jax.ShapeDtypeStruct((512, 2048), jnp.float32),
        ],
        scratch_shapes=[
            pltpu.VMEM((1280, 128), jnp.float32),
            pltpu.VMEM(square, jnp.float32),
            pltpu.VMEM(square, jnp.float32),
            pltpu.VMEM(square, jnp.float32),
            pltpu.VMEM(square, jnp.bfloat16),
            pltpu.VMEM(square, jnp.bfloat16),
            pltpu.VMEM((384, 1280), jnp.float32),
            pltpu.VMEM((4, 512, 512), jnp.float32),
            pltpu.VMEM((4, 512, 512), jnp.float32),
            pltpu.SemaphoreType.DMA((4,)),
            pltpu.SemaphoreType.DMA((4,)),
            pltpu.SemaphoreType.DMA((5,)),
            pltpu.SemaphoreType.DMA,
            pltpu.SemaphoreType.DMA((4,)),
        ],
        compiler_params=pltpu.CompilerParams(vmem_limit_bytes=60 * MIB),
        name="update",
    )(bmap, order, *l_parts, *a_parts, front, own, prev0, prev1, edge0, edge1, a_col)


def after(x, *earlier):
    return lax.optimization_barrier((x, *earlier))[0]


def body(front_matrix, child_update, bmap, order):
    front = front_matrix[0]
    child = child_update[0]
    row = lax.axis_index("row")
    c = lax.axis_index("col")

    ea, eb, e0, e1, top, bottom = pack_call(child)
    ee = permute(e1, lambda f, r, c: (f ^ 1, (r + 1) % ROWS, 0) if c == 3 else None)
    ed = permute(e0, lambda f, r, c: (f ^ 1, r, 0) if c == 3 else None)
    eb = permute(eb, lambda f, r, c: (f ^ 1, (r + 1) % ROWS, 0) if c == 0 else None)
    ea = permute(ea, lambda f, r, c: (f ^ 1, r, 0) if c == 0 else None)
    quarter = panel_call(bmap, order, front[:, :PANEL], ea, eb, ed, ee)

    def across(x):
        return permute(x, lambda f, r, c: (f ^ 1, r, c))

    top, bottom, _ = lax.optimization_barrier((top, bottom, quarter[0]))
    own = across(top)
    prev1 = permute(bottom, lambda f, r, c: (f, (r + 1) % ROWS, c))

    got = [
        permute(quarter[q], lambda f, r, c, q=q: (f, r, q) if c == 0 else None) for q in (1, 2, 3)
    ]

    half = first_call(quarter)
    *got, own, prev1, _ = lax.optimization_barrier((*got, own, prev1, half[0]))
    prev1 = across(prev1)
    mine = jnp.where(c == 0, quarter[0], got[0] + got[1] + got[2])

    piece = permute(mine, lambda f, r, c: (f, 4 * (r % 4) + c, r // 4))

    a_parts = [permute(mine, lambda f, r, c, s=s: (f, r, (c + s) % COLS)) for s in (1, 2, 3)]

    *half, _, _ = lax.optimization_barrier((*half, mine, own))
    part = second_call(*half)
    piece, prev1, own, e1, *part = lax.optimization_barrier(
        (piece, prev1, own, e1, *part, *a_parts)
    )
    part, a_parts = part[:4], [mine, *part[4:]]
    prev0 = permute(own, lambda f, r, c: (f, (r + 1) % ROWS, c))
    edge = permute(e1, lambda f, r, c: (f, r, (c + 1) % COLS))
    a_col = lax.all_gather(piece, "row", axis=0, tiled=True)

    got = [
        permute(part[q], lambda f, r, c, q=q: (f, 0, q) if r == 0 and c == 0 else None)
        for q in (1, 2, 3)
    ]
    d = jnp.where(c == 0, part[0], got[0] + got[1] + got[2])
    d1 = permute(d, lambda f, r, c: (f, 6, c) if r == 0 else None)
    d2 = permute(d, lambda f, r, c: (f, 12, c) if r == 0 else None)
    d = jnp.where(row == 0, d, d1 + d2)
    d, prev0, edge = lax.optimization_barrier((d, prev0, edge))
    edge0 = across(edge)
    d1 = permute(d, lambda f, r, c: (f, (r + 2) % ROWS, c) if r in (0, 6, 12) else None)
    d2 = permute(d, lambda f, r, c: (f, r - 2, c) if r in (6, 12) else None)
    d = jnp.where((row == 0) | (row == 6) | (row == 12), d, d1 + d2)
    d, edge0 = lax.optimization_barrier((d, edge0))
    edge1 = permute(edge0, lambda f, r, c: (f, (r + 1) % ROWS, c))
    d1 = permute(d, lambda f, r, c: (f, r + 1, c) if r % 2 == 0 else None)
    d = jnp.where(row % 2 == 0, d, d1)
    l_parts = [d] + [permute(d, lambda f, r, c, s=s: (f, r, (c + s) % COLS)) for s in (1, 2, 3)]

    x, s = update_call(bmap, order, l_parts, a_parts, front, own, prev0, prev1, edge0, edge1, a_col)
    return x[None], s[None]


def solution(mesh):
    return jax.shard_map(
        body,
        mesh=mesh,
        in_specs=(P("front", "row", "col"), P("front", "row", "col"), P("front", None), P("front")),
        out_specs=(P("front", "row", None), P("front", "row", "col")),
        check_vma=False,
    )
```

```python
import jax
import jax.numpy as jnp
from jax import lax
from jax.experimental import pallas as pl
from jax.experimental.pallas import tpu as pltpu
from jax.sharding import PartitionSpec as P

BLOCK = 128
PANEL = 512
FRONTS, ROWS, COLS = 4, 16, 4
AXES = ("front", "row", "col")
HIGHEST = lax.Precision.HIGHEST
MIB = 2**20


def permute(x, route):
    def flat(f, r, c):
        return (f * ROWS + r) * COLS + c

    pairs = []
    for f in range(FRONTS):
        for r in range(ROWS):
            for c in range(COLS):
                target = route(f, r, c)
                if target is not None:
                    pairs.append((flat(f, r, c), flat(*target)))
    return lax.ppermute(x, AXES, pairs)


def dot(a, b, ca, cb):
    return lax.dot_general(
        a, b, (((ca,), (cb,)), ((), ())), precision=HIGHEST, preferred_element_type=jnp.float32
    )


def smem():
    return pl.BlockSpec(memory_space=pltpu.SMEM)


def hbm():
    return pl.BlockSpec(memory_space=pltpu.HBM)


def whole(shape):
    return pl.BlockSpec(shape, lambda i: (0,) * len(shape))


def place(dst, col_off, bmap, run, rows, cols, tile):
    for row_id, row_part in rows:
        t = bmap[0, row_id]
        for col_id, fetch in cols:
            u = bmap[0, col_id]

            @pl.when((t // 4 == run) & (u // 4 == tile))
            def _():
                at_r = pl.ds(pl.multiple_of((t % 4) * BLOCK, BLOCK), BLOCK)
                at_c = pl.ds(pl.multiple_of(col_off + (u % 4) * BLOCK, BLOCK), BLOCK)
                dst[at_r, at_c] = dst[at_r, at_c] + fetch(row_part)


def pack_kernel(left, right, block, ea, eb, ed, ee, top, bottom):
    top[...] = block[:BLOCK, :]
    bottom[...] = block[BLOCK:, :]
    ea[...] = left[:BLOCK, :]
    eb[...] = left[...]
    ed[...] = right[:BLOCK, :]
    ee[...] = right[...]


def pack_call(child):
    shapes = [(128, 128), (256, 128), (128, 256), (256, 256), (128, 1024), (128, 1024)]
    return pl.pallas_call(
        pack_kernel,
        grid=(1,),
        in_specs=[
            pl.BlockSpec((256, 128), lambda i: (0, 0)),
            pl.BlockSpec((256, 256), lambda i: (0, 3)),
            pl.BlockSpec((256, 1024), lambda i: (0, 0)),
        ],
        out_specs=[whole(x) for x in shapes],
        out_shape=[jax.ShapeDtypeStruct(x, jnp.float32) for x in shapes],
        name="pack",
    )(child, child, child)


def panel_kernel(bmap, order, front, ea, eb, ed, ee, q0, q1, q2, q3, work):
    r = lax.axis_index("row")
    work[...] = front[...]

    def left(part):
        return ea[...] if part == 0 else eb[(part - 1) * BLOCK : part * BLOCK, :]

    def right(which):
        at = slice(which * BLOCK, (which + 1) * BLOCK)

        def fetch(part):
            return ed[:, at] if part == 0 else ee[(part - 1) * BLOCK : part * BLOCK, at]

        return fetch

    rows = [(2 * r, 0), ((2 * r + 30) % 32, 1), ((2 * r + 31) % 32, 2)]
    cols = [(0, left), (30, right(0)), (31, right(1))]
    place(work, 0, bmap, r, rows, cols, 0)
    for q, out in enumerate((q0, q1, q2, q3)):
        index = r * 512 + q * BLOCK + lax.broadcasted_iota(jnp.int32, out.shape, 0)
        out[...] = jnp.where(index < order[0], work[q * BLOCK : (q + 1) * BLOCK, :], 0.0)


def panel_call(bmap, order, front, *pieces):
    return pl.pallas_call(
        panel_kernel,
        grid=(1,),
        in_specs=[smem(), smem(), whole((512, 512))] + [whole(p.shape) for p in pieces],
        out_specs=[whole((128, 512))] * 4,
        out_shape=[jax.ShapeDtypeStruct((128, 512), jnp.float32)] * 4,
        scratch_shapes=[pltpu.VMEM((512, 512), jnp.float32)],
        compiler_params=pltpu.CompilerParams(vmem_limit_bytes=16 * MIB),
        name="panel",
    )(bmap, order, front, *pieces)


def reciprocal(d):
    r = pl.reciprocal(d, approx=True)
    return r * (2.0 - d * r)


def sweep(groups):
    lane = lax.broadcasted_iota(jnp.int32, (8, 128), 1)
    sub = lax.broadcasted_iota(jnp.int32, (8, 128), 0)
    w = list(groups)

    def across(v, k):
        return jnp.broadcast_to(v[:, k : k + 1], (8, 128))

    def down(v, k):
        return jnp.broadcast_to(v[k : k + 1, :], (8, 128))

    for g in range(16):
        base = 8 * g
        top = w[g]
        col = [across(top, base + j) for j in range(8)]
        inverse, pivot = [], {}
        for j in range(8):
            inverse.append(reciprocal(down(col[j], j)))
            m = jnp.where(sub > j, col[j] * inverse[j], 0.0)
            row = jnp.where(lane == base + j, 1.0, down(top, j))
            top = jnp.where((lane == base + j) & (sub > j), 0.0, top) - m * row
            for q in range(j + 1, 8):
                pivot[j, q] = down(col[q], j)
                col[q] = col[q] - m * pivot[j, q]
        w[g] = top
        inside = (lane >= base) & (lane < base + 8)
        rows = []
        for j in range(8):
            later = (lane > base + j) & (lane < base + 8)
            rows.append(jnp.where(lane == base + j, 1.0, jnp.where(later, 0.0, down(top, j))))
        for h in range(g + 1, 16):
            c = [across(w[h], base + j) for j in range(8)]
            acc = jnp.where(inside, 0.0, w[h])
            for j in range(8):
                m = c[j] * inverse[j]
                for q in range(j + 1, 8):
                    c[q] = c[q] - m * pivot[j, q]
                acc = acc - m * rows[j]
            w[h] = acc
    return w


def gather_rows(dst, parts):
    c = lax.axis_index("col")
    rows = dst.shape[0] // 4
    for s, p in enumerate(parts):
        at = pl.ds(pl.multiple_of(((c + 4 - s) % 4) * rows, rows), rows)
        dst[at, :] = p[...]


def invert(work, out, low):
    ri = lax.broadcasted_iota(jnp.int32, (BLOCK, BLOCK), 0)
    ci = lax.broadcasted_iota(jnp.int32, (BLOCK, BLOCK), 1)

    def step(j, carry):
        off = pl.multiple_of(j * BLOCK, BLOCK)
        groups = [
            work[pl.ds(pl.multiple_of(off + 8 * g, 8), 8), pl.ds(off, BLOCK)] for g in range(16)
        ]
        w = jnp.concatenate(sweep(groups), axis=0)
        scale = lax.rsqrt(jnp.sum(jnp.where(ri == ci, w, 0.0), axis=1, keepdims=True))
        inv = jnp.where(ri > ci, w, jnp.where(ri == ci, 1.0, 0.0)) * scale
        out[pl.ds(off, BLOCK), pl.ds(off, BLOCK)] = inv

        @pl.when(j == 0)
        def _():
            below = dot(work[BLOCK:, :BLOCK], inv, 1, 1)
            work[BLOCK:, BLOCK:] = work[BLOCK:, BLOCK:] - dot(below, below, 1, 1)
            low[...] = below

        @pl.when(j == 1)
        def _():
            out[BLOCK:, :BLOCK] = -dot(inv, dot(low[...], out[:BLOCK, :BLOCK], 1, 0), 1, 0)
            out[:BLOCK, BLOCK:] = jnp.zeros((BLOCK, BLOCK), jnp.float32)

        return carry

    lax.fori_loop(0, 2, step, 0)


HALF = (256, 256)


def first_kernel(q0, q1, q2, q3, inv, below, rest, work, low):
    work[:BLOCK, :] = q0[:, :256]
    work[BLOCK:, :] = q1[:, :256]
    invert(work, inv, low)
    x = dot(jnp.concatenate([q2[:, :256], q3[:, :256]], axis=0), inv[...], 1, 1)
    below[...] = x
    rest[...] = jnp.concatenate([q2[:, 256:], q3[:, 256:]], axis=0) - dot(x, x, 1, 1)


def first_call(quarter):
    return pl.pallas_call(
        first_kernel,
        grid=(1,),
        in_specs=[whole((128, 512))] * 4,
        out_specs=[whole(HALF)] * 3,
        out_shape=[jax.ShapeDtypeStruct(HALF, jnp.float32)] * 3,
        scratch_shapes=[pltpu.VMEM(HALF, jnp.float32), pltpu.VMEM((BLOCK, BLOCK), jnp.float32)],
        compiler_params=pltpu.CompilerParams(vmem_limit_bytes=16 * MIB),
        cost_estimate=pl.CostEstimate(flops=10**10, bytes_accessed=4 * MIB, transcendentals=0),
        name="first",
    )(*quarter)


def second_kernel(inv, below, rest, k0, k1, k2, k3, work, out, low, packed):
    work[...] = rest[...]
    invert(work, out, low)
    corner = -dot(out[...], dot(below[...], inv[...], 1, 0), 1, 0)
    spots = [(inv, 0, 0), (inv, 1, 0), (inv, 1, 1), (out, 0, 0), (out, 1, 0), (out, 1, 1)]
    for k, (src, i, j) in enumerate(spots):
        packed[k * BLOCK : (k + 1) * BLOCK, :] = src[
            i * BLOCK : (i + 1) * BLOCK, j * BLOCK : (j + 1) * BLOCK
        ]
    packed[768:1024, :] = corner[:, :BLOCK]
    packed[1024:, :] = corner[:, BLOCK:]
    for q, k in enumerate((k0, k1, k2, k3)):
        k[...] = packed[q * 320 : (q + 1) * 320, :]


def unpack(linv, packed):
    linv[...] = jnp.zeros_like(linv)
    for k, (i, j) in enumerate(((0, 0), (1, 0), (1, 1), (2, 2), (3, 2), (3, 3))):
        linv[i * BLOCK : (i + 1) * BLOCK, j * BLOCK : (j + 1) * BLOCK] = packed[
            k * BLOCK : (k + 1) * BLOCK, :
        ]
    linv[256:, :BLOCK] = packed[768:1024, :]
    linv[256:, BLOCK:256] = packed[1024:, :]


def second_call(inv, below, rest):
    part = (320, 128)
    return pl.pallas_call(
        second_kernel,
        grid=(1,),
        in_specs=[whole(HALF)] * 3,
        out_specs=[whole(part)] * 4,
        out_shape=[jax.ShapeDtypeStruct(part, jnp.float32)] * 4,
        scratch_shapes=[
            pltpu.VMEM(HALF, jnp.float32),
            pltpu.VMEM(HALF, jnp.float32),
            pltpu.VMEM((BLOCK, BLOCK), jnp.float32),
            pltpu.VMEM((1280, 128), jnp.float32),
        ],
        compiler_params=pltpu.CompilerParams(vmem_limit_bytes=16 * MIB),
        cost_estimate=pl.CostEstimate(flops=10**10, bytes_accessed=4 * MIB, transcendentals=0),
        name="second",
    )(inv, below, rest)


def halves(x):
    high = x.astype(jnp.bfloat16)
    return high, (x - high.astype(jnp.float32)).astype(jnp.bfloat16)


def dot3(a_high, a_low, b_high, b_low):
    def part(x, y):
        return lax.dot_general(
            x, y, (((1,), (1,)), ((), ())), preferred_element_type=jnp.float32
        )

    return part(a_high, b_high) + (part(a_high, b_low) + part(a_low, b_high))


def update_kernel(
    bmap, order, l0, l1, l2, l3, a0, a1, a2, a3, front, own, prev0, prev1, edge0, edge1, a_col,
    x_out, s_out, packed, linv, a_row, x_buf, z_high, z_low, child, tiles, cols, front_sem, col_sem, child_sem, x_sem, s_sem,
):
    r = lax.axis_index("row")
    c = lax.axis_index("col")
    wide = child.shape[1]

    def columns(t):
        return pl.ds(pl.multiple_of(t * 512, 512), 512)

    def front_copy(t):
        return pltpu.make_async_copy(front.at[:, columns(t)], tiles.at[t], front_sem.at[t])

    def col_copy(t):
        return pltpu.make_async_copy(a_col.at[columns(t), :], cols.at[t], col_sem.at[t])

    def out_copy(t):
        return pltpu.make_async_copy(tiles.at[t], s_out.at[:, columns(t)], s_sem.at[t])

    upper, rest = pl.ds(0, BLOCK), pl.ds(BLOCK, 2 * BLOCK)
    middle, lower = pl.ds(BLOCK, BLOCK), pl.ds(2 * BLOCK, BLOCK)
    left, right = pl.ds(0, 2 * BLOCK), pl.ds(2 * BLOCK, wide - 2 * BLOCK)
    child_copies = [
        pltpu.make_async_copy(src, child.at[at], child_sem.at[k])
        for k, (src, at) in enumerate(
            [
                (own, (upper, right)),
                (prev0, (middle, right)),
                (prev1, (lower, right)),
                (edge0.at[upper, :], (upper, left)),
                (edge1, (rest, left)),
            ]
        )
    ]
    front_copy(0).start()
    for copy in child_copies:
        copy.start()
    col_copy(0).start()
    for t in range(1, 4):
        front_copy(t).start()
        col_copy(t).start()

    gather_rows(packed, (l0, l1, l2, l3))
    unpack(linv, packed)
    gather_rows(a_row, (a0, a1, a2, a3))
    x = dot(a_row[...], linv[...], 1, 1)
    x_buf[...] = x
    x_copy = pltpu.make_async_copy(x_buf, x_out, x_sem)
    x_copy.start()
    high, low = halves(dot(x, linv[...], 1, 0))
    z_high[...] = high
    z_low[...] = low
    for copy in child_copies:
        copy.wait()

    rows = [(2 * r, 0), ((2 * r + 30) % 32, 1), ((2 * r + 31) % 32, 2)]
    row = r * 512 + lax.broadcasted_iota(jnp.int32, (512, 1), 0)

    def step(t, carry):
        front_copy(t).wait()
        tile = tiles.at[t]

        def block(k):
            at = pl.ds(pl.multiple_of((2 * t + k) * BLOCK, BLOCK), BLOCK)
            return lambda part: child[part * BLOCK : (part + 1) * BLOCK, at]

        ids = [((8 * c + 2 * t + 30 + k) % 32, block(k)) for k in range(3)]
        place(tile, 0, bmap, r, rows, ids, 4 * c + t)
        col_copy(t).wait()
        col = (4 * c + t) * 512 + lax.broadcasted_iota(jnp.int32, (1, 512), 1)
        keep = (row >= PANEL) & (row < order[0]) & (col >= PANEL) & (col < order[0])
        product = dot3(z_high[...], z_low[...], *halves(cols[t]))
        tile[...] = jnp.where(keep, tile[...] - product, 0.0)
        out_copy(t).start()
        return carry

    lax.fori_loop(0, 4, step, 0)
    x_copy.wait()
    for t in range(4):
        out_copy(t).wait()


def update_call(bmap, order, l_parts, a_parts, front, own, prev0, prev1, edge0, edge1, a_col):
    square = (512, 512)
    return pl.pallas_call(
        update_kernel,
        grid=(1,),
        in_specs=[smem(), smem()]
        + [whole((320, 128))] * 4
        + [whole((128, 512))] * 4
        + [hbm()] * 7,
        out_specs=[hbm(), hbm()],
        out_shape=[
            jax.ShapeDtypeStruct(square, jnp.float32),
            jax.ShapeDtypeStruct((512, 2048), jnp.float32),
        ],
        scratch_shapes=[
            pltpu.VMEM((1280, 128), jnp.float32),
            pltpu.VMEM(square, jnp.float32),
            pltpu.VMEM(square, jnp.float32),
            pltpu.VMEM(square, jnp.float32),
            pltpu.VMEM(square, jnp.bfloat16),
            pltpu.VMEM(square, jnp.bfloat16),
            pltpu.VMEM((384, 1280), jnp.float32),
            pltpu.VMEM((4, 512, 512), jnp.float32),
            pltpu.VMEM((4, 512, 512), jnp.float32),
            pltpu.SemaphoreType.DMA((4,)),
            pltpu.SemaphoreType.DMA((4,)),
            pltpu.SemaphoreType.DMA((5,)),
            pltpu.SemaphoreType.DMA,
            pltpu.SemaphoreType.DMA((4,)),
        ],
        compiler_params=pltpu.CompilerParams(vmem_limit_bytes=60 * MIB),
        name="update",
    )(bmap, order, *l_parts, *a_parts, front, own, prev0, prev1, edge0, edge1, a_col)


def after(x, *earlier):
    return lax.optimization_barrier((x, *earlier))[0]


def body(front_matrix, child_update, bmap, order):
    front = front_matrix[0]
    child = child_update[0]
    row = lax.axis_index("row")
    c = lax.axis_index("col")

    ea, eb, e0, e1, top, bottom = pack_call(child)
    ee = permute(e1, lambda f, r, c: (f ^ 1, (r + 1) % ROWS, 0) if c == 3 else None)
    ed = permute(e0, lambda f, r, c: (f ^ 1, r, 0) if c == 3 else None)
    eb = permute(eb, lambda f, r, c: (f ^ 1, (r + 1) % ROWS, 0) if c == 0 else None)
    ea = permute(ea, lambda f, r, c: (f ^ 1, r, 0) if c == 0 else None)
    quarter = panel_call(bmap, order, front[:, :PANEL], ea, eb, ed, ee)

    def across(x):
        return permute(x, lambda f, r, c: (f ^ 1, r, c))

    top, bottom, _ = lax.optimization_barrier((top, bottom, quarter[0]))
    own = across(top)
    prev1 = permute(bottom, lambda f, r, c: (f, (r + 1) % ROWS, c))

    got = [
        permute(quarter[q], lambda f, r, c, q=q: (f, r, q) if c == 0 else None) for q in (1, 2, 3)
    ]

    half = first_call(quarter)
    *got, own, prev1, _ = lax.optimization_barrier((*got, own, prev1, half[0]))
    prev1 = across(prev1)
    mine = jnp.where(c == 0, quarter[0], got[0] + got[1] + got[2])

    piece = permute(mine, lambda f, r, c: (f, 4 * (r % 4) + c, r // 4))

    a_parts = [permute(mine, lambda f, r, c, s=s: (f, r, (c + s) % COLS)) for s in (1, 2, 3)]

    *half, _, _ = lax.optimization_barrier((*half, mine, own))
    part = second_call(*half)
    piece, prev1, own, e1, *part = lax.optimization_barrier(
        (piece, prev1, own, e1, *part, *a_parts)
    )
    part, a_parts = part[:4], [mine, *part[4:]]
    prev0 = permute(own, lambda f, r, c: (f, (r + 1) % ROWS, c))
    edge = permute(e1, lambda f, r, c: (f, r, (c + 1) % COLS))
    a_col = lax.all_gather(piece, "row", axis=0, tiled=True)

    got = [
        permute(part[q], lambda f, r, c, q=q: (f, 0, q) if r == 0 and c == 0 else None)
        for q in (1, 2, 3)
    ]
    d = jnp.where(c == 0, part[0], got[0] + got[1] + got[2])
    d1 = permute(d, lambda f, r, c: (f, 6, c) if r == 0 else None)
    d2 = permute(d, lambda f, r, c: (f, 12, c) if r == 0 else None)
    d = jnp.where(row == 0, d, d1 + d2)
    d, prev0, edge = lax.optimization_barrier((d, prev0, edge))
    edge0 = across(edge)
    d1 = permute(d, lambda f, r, c: (f, (r + 2) % ROWS, c) if r in (0, 6, 12) else None)
    d2 = permute(d, lambda f, r, c: (f, r - 2, c) if r in (6, 12) else None)
    d = jnp.where((row == 0) | (row == 6) | (row == 12), d, d1 + d2)
    d, edge0 = lax.optimization_barrier((d, edge0))
    edge1 = permute(edge0, lambda f, r, c: (f, (r + 1) % ROWS, c))
    d1 = permute(d, lambda f, r, c: (f, r + 1, c) if r % 2 == 0 else None)
    d = jnp.where(row % 2 == 0, d, d1)
    l_parts = [d] + [permute(d, lambda f, r, c, s=s: (f, r, (c + s) % COLS)) for s in (1, 2, 3)]

    x, s = update_call(bmap, order, l_parts, a_parts, front, own, prev0, prev1, edge0, edge1, a_col)
    return x[None], s[None]


def solution(mesh):
    return jax.shard_map(
        body,
        mesh=mesh,
        in_specs=(P("front", "row", "col"), P("front", "row", "col"), P("front", None), P("front")),
        out_specs=(P("front", "row", None), P("front", "row", "col")),
        check_vma=False,
    )
```
